256 devices in a mesh: prompt: 16 (over y, x), member: 16 (over z, core).
Axes of the slice: x: 4, y: 4, z: 8, core: 2. Of those that a mesh axis runs over, the one named last changes fastest.
Arguments:
- queries: bfloat16 [16, 2048, 4096], P('prompt', 'member'), may hold values from -6 to 6
- out_grad: bfloat16 [16, 2048, 4096], P('prompt', 'member'), may hold values from -6 to 6
- log_norms: float32 [16, 32, 2048], P('prompt', None, 'member'), may hold values from 5.5 to 7.5
- row_deltas: float32 [16, 32, 2048], P('prompt', None, 'member'), may hold values from -8 to 8
- prompt_kv: bfloat16 [16, 2, 2048, 256], P('prompt', None, 'member'), may hold values from -6 to 6
- grad_rows: bfloat16 [2048, 4096], P('prompt', 'member'), may hold values from -1.1953125 to 1.1953125
- hidden_acts: bfloat16 [2048, 8, 1536], P('prompt'), may hold values from -6 to 6
- route_weight: float32 [2048, 8], P('prompt'), may hold values from 0.02 to 0.5
- expert_ids: int32 [2048, 8], P('prompt'), may hold values from 0 to 63, all different within a row; in each aligned block of 128 rows (0 to 127, 128 to 255, ...) at most 32 rows name the same one
- w_down: bfloat16 [64, 1536, 4096], P('prompt', None, 'member'), may hold values from -0.15625 to 0.15625
Outputs:
- query_grad: bfloat16 [16, 2048, 4096], P('prompt', 'member')
- prompt_kv_grad: float32 [16, 2, 2048, 256], P('prompt', None, 'member')
- w_down_grad: bfloat16 [64, 1536, 4096], P('prompt', None, 'member')
- route_grad: float32 [2048, 8], P('prompt')
The draws below stay inside these ranges and needn't reach their ends.
Inputs may be any that keep to these rules, and one draw needn't show every extreme that they name: `expert_ids`: within each aligned block of 128 rows (the rows of one prompt group) the 8 experts of a row differ, no expert is named by more than 32 rows of the block, a bound that some block reaches; every expert is named somewhere.
All inputs are finite; a program needn't handle non-finite values.
Results may differ from the reference program's by a relative error of at most 0.0057.
Values may be sent and summed in bfloat16 or wider, within the bound.
No kernel may reach another device: no remote copies, remote signals or barrier semaphores. Data moves between devices by JAX's collectives and lax.ppermute only.
A program may use at most 192 MiB of HBM per device.

```python
import math
import jax
import jax.numpy as jnp
import numpy as np
from jax import lax

D = 4096
QH = 32
KVH = 2
HD = 128
EFF = 1536
TOPK = 8
CAP = 32
PROMPTS = 16
EXPERTS = 64
RESP_ROWS = 2048
PLEN = 2048
G_TOK = 128
MOE_ROWS = 2048
N_PROMPT = 16


def level_of(stream_key, dims, cuts, least, top_value):
    def one(position, shards_of):
        draws = jax.random.uniform(jax.random.fold_in(jax.random.fold_in(stream_key, 6), position), (shards_of,), jnp.float32, least / len(cuts), top_value / len(cuts))
        return jnp.repeat(jnp.exp(draws), dims[position] // shards_of).reshape((-1,) + (1,) * (len(dims) - position - 1))

    loudness = one(*cuts[0])
    for cut in cuts[1:]:
        loudness = loudness * one(*cut)
    return loudness


def deal_out(rng, own, number, rows, amount, top, bound, lean):
    ranking = jax.random.permutation(rng, amount)
    heavy_load, usual = shares(amount, rows * top, bound, lean, True), shares(amount, rows * top, bound, lean, False)
    places = jnp.arange(amount)

    def named(sizes, rotation):
        used = int((sizes > 0).sum())
        fixed = max(1, used // 4)
        moved = fixed + (places - fixed + rotation * (used - fixed)) % max(1, amount - fixed)
        return jnp.zeros((amount,), jnp.int32).at[ranking[jnp.where(places < fixed, places, moved)]].set(jnp.asarray(sizes, jnp.int32))

    sizes = jnp.where(number % 4 == 0, named(heavy_load, number // 4), named(usual, number - number // 4 - 1))
    mixed = jax.random.permutation(jax.random.fold_in(own, 3), amount)
    giver, receiver = mixed[0:amount // 2 * 2:2], mixed[1:amount // 2 * 2:2]
    slack = jnp.minimum(sizes[giver] - 1, bound - sizes[receiver]) // 2
    slack = jnp.where((giver == ranking[0]) | (receiver == ranking[0]) | (sizes[receiver] == 0), 0, jnp.maximum(slack, 0))
    moved = jax.random.randint(jax.random.fold_in(own, 4), (amount // 2,), 0, 1 << 20) % (slack + 1)
    sizes = sizes.at[giver].add(-moved).at[receiver].add(moved)
    items = jnp.searchsorted(jnp.cumsum(sizes), jnp.arange(rows * top), side="right").astype(jnp.int32)
    table = items.reshape(top, rows).T
    table = table[jax.random.permutation(jax.random.fold_in(own, 1), rows)]
    rotation = jax.random.randint(jax.random.fold_in(own, 2), (rows, 1), 0, top)
    return jnp.take_along_axis(table, (jnp.arange(top)[None, :] + rotation) % top, axis=1)


def shares(count, total, reach, slope, full):
    portions = [(1 << 20) // math.isqrt(standing ** slope) + 1 for standing in range(1, count + 1)]
    largest = reach if full else min(reach, max(-(-total // count), total * portions[0] // sum(portions)))
    least = 1 if total - largest >= count - 1 else 0
    given, surplus = [largest] + [least] * (count - 1), total - largest - least * (count - 1)
    while surplus > 0:
        candidates = [i for i in range(1, count) if given[i] < largest] or [i for i in range(1, count) if given[i] < reach]
        whole, budget = sum([portions[i] for i in candidates]), surplus
        for i in candidates:
            extra = min(reach - given[i], max(1, budget * portions[i] // whole), surplus)
            given[i] = given[i] + extra
            surplus = surplus - extra
    return np.array(given)


def gaussian(stream_key, extent, spread, bound, pieces=(), held_as=jnp.bfloat16):
    level = level_of(stream_key, extent, pieces, -0.22, 0.18) if pieces else 1.0
    result = jax.random.normal(stream_key, extent, jnp.float32) * spread * level
    return jnp.minimum(jnp.maximum(result, -bound), bound).astype(held_as)


def setup_inputs(seed: int = 0) -> dict:
    streams_of = jax.random.split(jax.random.key(seed), 11)
    queries = gaussian(streams_of[0], (PROMPTS, RESP_ROWS, QH * HD), 1.0, 6.0, ((0, 16), (1, 16)))
    out_grad = gaussian(streams_of[1], (PROMPTS, RESP_ROWS, QH * HD), 1.0, 6.0, ((0, 16), (1, 16)))
    log_norms = jnp.clip(5.5 + 2.0 * jax.random.uniform(streams_of[2], (PROMPTS, QH, RESP_ROWS), jnp.float32) ** level_of(streams_of[2], (PROMPTS, QH, RESP_ROWS), ((0, 16), (2, 16)), -0.2, 0.2), 5.5, 7.5)
    row_deltas = gaussian(streams_of[3], (PROMPTS, QH, RESP_ROWS), 2.0, 8.0, ((0, 16), (2, 16)), jnp.float32)
    prompt_kv = gaussian(streams_of[4], (PROMPTS, 2, PLEN, KVH * HD), 1.0, 6.0, ((0, 16), (2, 16)))
    grad_rows = gaussian(streams_of[5], (MOE_ROWS, D), 0.2, 1.1953125, ((0, 16), (1, 16)))
    hidden_acts = gaussian(streams_of[6], (MOE_ROWS, TOPK, EFF), 1.0, 6.0, ((0, 16),))
    route_weight = jnp.clip(jnp.exp(math.log(0.5) - 3.218876 * jax.random.uniform(streams_of[7], (MOE_ROWS, TOPK), jnp.float32) ** level_of(streams_of[7], (MOE_ROWS, TOPK), ((0, 16),), -0.2, 0.2)), 0.02, 0.5)
    expert_ids_keys = jax.random.split(jax.random.fold_in(streams_of[8], 1), MOE_ROWS // G_TOK)
    expert_ids_turns = jax.random.permutation(jax.random.fold_in(streams_of[8], 3), MOE_ROWS // G_TOK)
    expert_ids = jax.vmap(lambda own, number: deal_out(jax.random.fold_in(streams_of[8], 2), own, number, G_TOK, EXPERTS, TOPK, CAP, 2))(expert_ids_keys, expert_ids_turns).reshape((MOE_ROWS, TOPK))
    w_down = gaussian(streams_of[9], (EXPERTS, EFF, D), EFF ** -0.5, 0.15625, ((0, 16), (2, 16)))
    return {"queries": queries, "out_grad": out_grad, "log_norms": log_norms, "row_deltas": row_deltas, "prompt_kv": prompt_kv, "grad_rows": grad_rows, "hidden_acts": hidden_acts, "route_weight": route_weight, "expert_ids": expert_ids, "w_down": w_down}


def reference(queries, out_grad, log_norms, row_deltas, prompt_kv, grad_rows, hidden_acts, route_weight, expert_ids, w_down):
    scale = HD ** -0.5
    group = QH // KVH

    def one_prompt(operands):
        query_block, grad_block, norm_block, delta_block, kv_block = operands
        key_heads = kv_block[0].reshape(PLEN, KVH, HD)
        value_heads = kv_block[1].reshape(PLEN, KVH, HD)
        query_heads = query_block.reshape(RESP_ROWS, QH, HD)
        grad_heads = grad_block.reshape(RESP_ROWS, QH, HD)

        def head_step(totals, head):
            key_grad, value_grad = totals
            kv_head = head // group
            key_mat = lax.dynamic_index_in_dim(key_heads, kv_head, 1, keepdims=False)
            value_mat = lax.dynamic_index_in_dim(value_heads, kv_head, 1, keepdims=False)
            query_mat = lax.dynamic_index_in_dim(query_heads, head, 1, keepdims=False)
            grad_mat = lax.dynamic_index_in_dim(grad_heads, head, 1, keepdims=False)
            norm_row = lax.dynamic_index_in_dim(norm_block, head, 0, keepdims=False)
            delta_row = lax.dynamic_index_in_dim(delta_block, head, 0, keepdims=False)
            scores = jnp.dot(query_mat, key_mat.T, preferred_element_type=jnp.float32) * scale
            probs = jnp.exp(scores - norm_row[:, None])
            probs_low = probs.astype(jnp.bfloat16)
            value_term = jnp.dot(probs_low.T, grad_mat, preferred_element_type=jnp.float32)
            dprob = jnp.dot(grad_mat, value_mat.T, preferred_element_type=jnp.float32)
            dscore = (scale * probs * (dprob - delta_row[:, None])).astype(jnp.bfloat16)
            query_term = jnp.dot(dscore, key_mat, preferred_element_type=jnp.float32)
            key_term = jnp.dot(dscore.T, query_mat, preferred_element_type=jnp.float32)
            key_grad = key_grad.at[:, kv_head].add(key_term)
            value_grad = value_grad.at[:, kv_head].add(value_term)
            return (key_grad, value_grad), query_term.astype(jnp.bfloat16)

        start_totals = (jnp.zeros((PLEN, KVH, HD), jnp.float32), jnp.zeros((PLEN, KVH, HD), jnp.float32))
        totals, query_terms = lax.scan(head_step, start_totals, jnp.arange(QH))
        query_out = jnp.transpose(query_terms, (1, 0, 2)).reshape(RESP_ROWS, QH * HD)
        kv_out = jnp.stack([totals[0].reshape(PLEN, KVH * HD), totals[1].reshape(PLEN, KVH * HD)])
        return query_out, kv_out

    query_grad, prompt_kv_grad = lax.map(one_prompt, (queries, out_grad, log_norms, row_deltas, prompt_kv))

    route_count = MOE_ROWS * TOPK
    flat_ids = expert_ids.reshape(-1)
    flat_hidden = hidden_acts.reshape(route_count, EFF)
    token_of_route = jnp.arange(route_count) // TOPK
    weight_low = route_weight.astype(jnp.bfloat16).astype(jnp.float32).reshape(-1)
    limit = N_PROMPT * CAP

    def expert_step(route_total, expert):
        chosen = flat_ids == expert
        picked = jnp.nonzero(chosen, size=limit, fill_value=0)[0]
        live = jnp.arange(limit) < jnp.sum(chosen.astype(jnp.int32))
        hidden_sel = flat_hidden[picked] * live[:, None].astype(flat_hidden.dtype)
        grad_sel = grad_rows[token_of_route[picked]]
        scaled = (weight_low[picked][:, None] * grad_sel.astype(jnp.float32)).astype(jnp.bfloat16)
        weight_grad = jnp.dot(hidden_sel.T, scaled, preferred_element_type=jnp.float32).astype(jnp.bfloat16)
        expert_out = jnp.dot(hidden_sel, w_down[expert], preferred_element_type=jnp.float32)
        dots = jnp.sum(expert_out * grad_sel.astype(jnp.float32), axis=1)
        route_total = route_total.at[picked].add(jnp.where(live, dots, jnp.zeros((), jnp.float32)))
        return route_total, weight_grad

    route_flat, w_down_grad = lax.scan(expert_step, jnp.zeros((route_count,), jnp.float32), jnp.arange(EXPERTS))
    route_grad = route_flat.reshape(MOE_ROWS, TOPK)
    return query_grad, prompt_kv_grad, w_down_grad, route_grad
```

```python
import functools
import math

import jax
import jax.numpy as jnp
from jax import lax
from jax.experimental import pallas as pl
from jax.experimental.pallas import tpu as pltpu
from jax.sharding import Mesh, PartitionSpec as P

QH = 32
KVH = 2
HD = 128
GROUP = QH // KVH
EFF = 1536
HALF = EFF // 2
TOPK = 8
CAP = 32
TOK = 128
ROUTES = TOK * TOPK
LOCAL = 4
EXPERTS = 64
SLOTS = LOCAL * CAP
DSTS = 4
NP = 16
NZ = 8
WID = 256
SCALE = HD ** (-0.5)
LOG2E = math.log2(math.e)
BF = jnp.bfloat16
F32 = jnp.float32
VMEM = 60 << 20
HEADS = 4
SWAP = [(0, 1), (1, 0)]


def shift(n, by):
    return [(i, (i + by) % n) for i in range(n)]


def cost(flops, moved, exps=0):
    return pl.CostEstimate(flops=flops, bytes_accessed=moved, transcendentals=exps)


def dot(a, b, ca=1, cb=0):
    return lax.dot_general(a, b, (((ca,), (cb,)), ((), ())), preferred_element_type=F32)


def iota(shape, dim):
    return lax.broadcasted_iota(jnp.int32, shape, dim)


def upper(n):
    return (iota((n, n), 0) < iota((n, n), 1)).astype(BF)


def dispatch_kernel(
    c_ref, ids_ref, w_ref, grad_ref, hid_ref, down_ref, out_ref, slot_ref, give_ref, row_ref
):
    give_ref[...] = down_ref[...]

    @pl.when(pl.program_id(0) == 0)
    def _():
        ids = ids_ref[...]
        hots = [(ids[k : k + 1] == iota((EXPERTS, TOK), 0)).astype(F32) for k in range(TOPK)]
        before = dot(sum(hots).astype(BF), upper(TOK))
        place = jnp.concatenate(
            [jnp.sum(h * before, axis=0, keepdims=True) for h in hots], axis=0
        )
        slot_ref[...] = ids * CAP + place.astype(jnp.int32)
        token = (iota((TOK, ROUTES), 0) == iota((TOK, ROUTES), 1) // TOPK).astype(F32).astype(BF)
        choice = (iota((TOPK, ROUTES), 0) == iota((TOPK, ROUTES), 1) % TOPK).astype(F32)
        wide = dot(ids.astype(F32).astype(BF), token) * CAP + dot(place.astype(BF), token)
        row_ref[...] = jnp.sum(wide * choice, axis=0, keepdims=True).astype(jnp.int32)

    slot = slot_ref[...]
    row = row_ref[...]
    weight = w_ref[...].astype(BF).astype(F32)
    for b in range(DSTS // 2):
        first = (pl.program_id(0) * DSTS + 2 * b) * SLOTS
        pick = (row == iota((2 * SLOTS, ROUTES), 0) + first).astype(F32).astype(BF)
        rows = dot(pick, hid_ref[...]).astype(BF)
        out_ref[2 * b : 2 * b + 2, :, :HALF] = rows.reshape(2, SLOTS, HALF)
        mine = iota((2 * SLOTS, TOK), 0) + first
        scale = jnp.zeros((2 * SLOTS, TOK), F32)
        for k in range(TOPK):
            scale = jnp.where(slot[k : k + 1] == mine, weight[k : k + 1], scale)
        scaled = dot(scale.astype(BF), grad_ref[...]).astype(BF)
        out_ref[2 * b : 2 * b + 2, :, HALF:] = scaled.reshape(2, SLOTS, WID)


def dispatch(core, ids_cols, weight_cols, grad_rows, hidden, w_down):
    small = pl.BlockSpec((TOPK, TOK), lambda j, c: (0, 0))
    return pl.pallas_call(
        dispatch_kernel,
        out_shape=(
            jax.ShapeDtypeStruct((NP, SLOTS, HALF + WID), BF),
            jax.ShapeDtypeStruct((TOPK, TOK), jnp.int32),
            jax.ShapeDtypeStruct((LOCAL, HALF, WID), BF),
        ),
        grid_spec=pltpu.PrefetchScalarGridSpec(
            num_scalar_prefetch=1,
            grid=(NP // DSTS,),
            in_specs=[
                small,
                small,
                pl.BlockSpec((TOK, WID), lambda j, c: (0, 0)),
                pl.BlockSpec((ROUTES, HALF), lambda j, c: (0, c[0])),
                pl.BlockSpec((1, HALF, WID), lambda j, c: (j, 1 - c[0], 0)),
            ],
            out_specs=(
                pl.BlockSpec((DSTS, SLOTS, HALF + WID), lambda j, c: (j, 0, 0)),
                small,
                pl.BlockSpec((1, HALF, WID), lambda j, c: (j, 0, 0)),
            ),
            scratch_shapes=[pltpu.VMEM((1, ROUTES), jnp.int32)],
        ),
        compiler_params=pltpu.CompilerParams(vmem_limit_bytes=VMEM),
        cost_estimate=cost(2 * NP * SLOTS * ROUTES * HALF, 6 << 20),
        name="dispatch",
    )(core, ids_cols, weight_cols, grad_rows, hidden, w_down)


def expert_kernel(c_ref, got_ref, ssib_ref, wown_ref, wsib_ref, dots_ref, own_ref, sib_ref):
    hid = got_ref[:, :, :HALF].reshape(NP * CAP, HALF)
    total = jnp.zeros((NP * CAP, HD), F32)
    for scl, w, out in (
        (got_ref[:, :, HALF:], wown_ref[0], own_ref),
        (ssib_ref[...], wsib_ref[0], sib_ref),
    ):
        scl = scl.reshape(NP * CAP, WID)
        prod = dot(hid, w) * scl.astype(F32)
        total = total + prod[:, :HD] + prod[:, HD:]
        out[0] = dot(hid, scl, 0, 0).astype(BF)
    dots_ref[0] = jnp.sum(total.T, axis=0, keepdims=True)


def experts(core, got, scl_sib, w_down, w_sib):
    half = pl.BlockSpec((1, HALF, WID), lambda e, c: (e, c[0], 0))
    return pl.pallas_call(
        expert_kernel,
        out_shape=(
            jax.ShapeDtypeStruct((LOCAL, 1, NP * CAP), F32),
            jax.ShapeDtypeStruct((LOCAL, EFF, WID), BF),
            jax.ShapeDtypeStruct((LOCAL, HALF, WID), BF),
        ),
        grid_spec=pltpu.PrefetchScalarGridSpec(
            num_scalar_prefetch=1,
            grid=(LOCAL,),
            in_specs=[
                pl.BlockSpec((NP, CAP, HALF + WID), lambda e, c: (0, e, 0)),
                pl.BlockSpec((NP, CAP, WID), lambda e, c: (0, e, 0)),
                half,
                pl.BlockSpec((1, HALF, WID), lambda e, c: (e, 0, 0)),
            ],
            out_specs=(
                pl.BlockSpec((1, 1, NP * CAP), lambda e, c: (e, 0, 0)),
                half,
                pl.BlockSpec((1, HALF, WID), lambda e, c: (e, 0, 0)),
            ),
        ),
        compiler_params=pltpu.CompilerParams(vmem_limit_bytes=VMEM),
        cost_estimate=cost(4 * LOCAL * 512 * HALF * 512, 13 << 20),
        name="experts",
    )(core, got, scl_sib, w_down, w_sib)


def join_kernel(c_ref, whole_ref, part_ref, out_ref):
    out_ref[...] = part_ref[...]


def join(core, whole, part, grid, block, whole_at, part_at, name):
    return pl.pallas_call(
        join_kernel,
        out_shape=jax.ShapeDtypeStruct(whole.shape, whole.dtype),
        grid_spec=pltpu.PrefetchScalarGridSpec(
            num_scalar_prefetch=1,
            grid=grid,
            in_specs=[pl.BlockSpec(memory_space=pl.ANY), pl.BlockSpec(block, part_at)],
            out_specs=pl.BlockSpec(block, whole_at),
        ),
        input_output_aliases={1: 0},
        compiler_params=pltpu.CompilerParams(vmem_limit_bytes=8 << 20),
        cost_estimate=cost(0, 2 * part.size * 2),
        name=name,
    )(core, whole, part)


def attend_kernel(first, last, *refs):
    c_ref, q_own, q_sib, g_own, g_sib, n_own, n_sib, d_own, d_sib, chunks = refs[:10]
    refs = refs[10:]
    if not first:
        dq_in, refs = refs[0], refs[1:]
    if last:
        dkv_out, dq_own, dq_sib, acc = refs
    else:
        dkv_out, dq_out, acc = refs
    step = pl.program_id(0)

    @pl.when(step == 0)
    def _():
        acc[...] = jnp.zeros_like(acc)

    heads = range(HEADS)
    cols = [slice(i * HD, (i + 1) * HD) for i in heads]
    q = jnp.concatenate([r[0, :, s] for s in cols for r in (q_own, q_sib)], axis=0)
    g = jnp.concatenate([r[0, :, s] for s in cols for r in (g_own, g_sib)], axis=0)

    def rows(own, sib):
        parts = []
        for i in heads:
            h = c_ref[0] * GROUP + step * HEADS + i
            parts += [own[0, pl.ds(h, 1), :], sib[0, pl.ds(h, 1), :]]
        return jnp.concatenate(parts, axis=1)

    norm = rows(n_own, n_sib) * LOG2E - math.log2(SCALE)
    delta = rows(d_own, d_sib)
    total = None
    for i in range(chunks.shape[0]):
        k, v = chunks[i, 0], chunks[i, 1]
        probs = jnp.exp2(dot(k, q, 1, 1) * (SCALE * LOG2E) - norm)
        dscore = (probs * (dot(v, g, 1, 1) - delta)).astype(BF)
        acc[i, 0] += dot(dscore, q)
        acc[i, 1] += dot(probs.astype(BF), g)
        term = dot(k, dscore, 0, 0)
        total = term if total is None else total + term
    total = total.T
    for i in heads:
        piece = total[i * 2 * HD : (i + 1) * 2 * HD]
        if not first:
            piece = piece + dq_in[:, cols[i]]
        if last:
            dq_own[0, :, cols[i]] = piece[:HD].astype(BF)
            dq_sib[:, cols[i]] = piece[HD:].astype(BF)
        else:
            dq_out[:, cols[i]] = piece

    @pl.when(step == GROUP // HEADS - 1)
    def _():
        dkv_out[:, 0] = acc[:, 0].astype(dkv_out.dtype)
        dkv_out[:, 1] = (acc[:, 1] * (1.0 / SCALE)).astype(dkv_out.dtype)


def attend(core, rows, chunks, kind, dq=None, last=False):
    first = dq is None
    count = chunks.shape[0]
    span = HEADS * HD
    wide = pl.BlockSpec((1, HD, span), lambda h, c: (0, 0, c[0] * (GROUP // HEADS) + h))
    line = pl.BlockSpec((1, QH, HD), lambda h, c: (0, 0, 0))
    keys = pl.BlockSpec(chunks.shape, lambda h, c: (0, 0, 0, 0))
    both = pl.BlockSpec((2 * HD, span), lambda h, c: (0, h))
    one = pl.BlockSpec((HD, span), lambda h, c: (0, h))
    in_specs = [wide] * 4 + [line] * 4 + [keys]
    args = [arr for pair in rows for arr in pair] + [chunks]
    outs = [jax.ShapeDtypeStruct(chunks.shape, kind)]
    out_specs = [keys]
    if not first:
        in_specs.append(both)
        args.append(dq)
    if last:
        outs += [
            jax.ShapeDtypeStruct((1, HD, QH * HD), BF),
            jax.ShapeDtypeStruct((HD, GROUP * HD), BF),
        ]
        out_specs += [wide, one]
    else:
        outs += [jax.ShapeDtypeStruct((2 * HD, GROUP * HD), F32)]
        out_specs += [both]
    return pl.pallas_call(
        functools.partial(attend_kernel, first, last),
        out_shape=tuple(outs),
        grid_spec=pltpu.PrefetchScalarGridSpec(
            num_scalar_prefetch=1,
            grid=(GROUP // HEADS,),
            in_specs=in_specs,
            out_specs=tuple(out_specs),
            scratch_shapes=[pltpu.VMEM(chunks.shape, F32)],
        ),
        compiler_params=pltpu.CompilerParams(vmem_limit_bytes=VMEM),
        cost_estimate=cost(
            10 * count * GROUP * 256 * 256 * 256, 8 << 20, count * GROUP * 256 * 256
        ),
        name=f"attend_{count}",
    )(core, *args)


def collect_kernel(slot_ref, w_ref, got_ref, out_ref):
    turned = jnp.sum(got_ref[...].reshape(NP, NZ, SLOTS), axis=1).T
    for k in range(TOPK):
        slot = slot_ref[k : k + 1, :]
        total = jnp.zeros((8, TOK), F32)
        for p in range(NP):
            want = iota((SLOTS, TOK), 0) + p * SLOTS
            hit = jnp.where(slot == want, turned[:, p : p + 1], 0.0)
            total = total + jnp.sum(hit.reshape(SLOTS // 8, 8, TOK), axis=0)
        out_ref[k : k + 1, :] = jnp.sum(total, axis=0, keepdims=True)
    out_ref[...] = out_ref[...] / w_ref[...].astype(BF).astype(F32)


def collect(slot, weight_cols, got):
    return pl.pallas_call(
        collect_kernel,
        out_shape=jax.ShapeDtypeStruct((TOPK, TOK), F32),
        compiler_params=pltpu.CompilerParams(vmem_limit_bytes=VMEM),
        cost_estimate=cost(8 << 20, 1 << 18),
        name="collect",
    )(slot, weight_cols, got)


def body(
    queries,
    out_grad,
    log_norms,
    row_deltas,
    prompt_kv,
    grad_rows,
    hidden_acts,
    route_weight,
    expert_ids,
    w_down,
):
    c = lax.axis_index("c")
    core = c.astype(jnp.int32)[None]
    prompt = lax.axis_index("prompt").astype(jnp.int32)[None]

    def swap(x):
        return lax.ppermute(x, "c", SWAP)

    def across(x, by):
        return lax.ppermute(x, "z", [(i, i ^ by) for i in range(NZ)])

    own = jnp.concatenate([prompt_kv[0], swap(prompt_kv[0])], axis=1)
    own = jnp.where(c == 0, own[:, :, :HD], own[:, :, HD:])[None]

    ids_cols, weight_cols = expert_ids.T, route_weight.T
    sent, slot, w_give = dispatch(
        core, ids_cols, weight_cols, grad_rows, hidden_acts.reshape(ROUTES, EFF), w_down
    )
    sibs = [swap(x) for x in (queries, out_grad, log_norms, row_deltas)]
    sent, sibs, own = lax.optimization_barrier((sent, sibs, own))
    rows = list(zip((queries, out_grad, log_norms, row_deltas), sibs))
    got = lax.all_to_all(sent, "prompt", 0, 0, tiled=True)
    keys = [own] + [across(own, k) for k in (4, 2, 6)]
    keys_a = jnp.concatenate(keys[:2], axis=0)
    keys_c = jnp.concatenate(keys[2:], axis=0)
    keys_b = across(jnp.concatenate([keys_a, keys_c], axis=0), 1)
    w_sib = swap(w_give)

    kv_a, dq = attend(core, rows, keys_a, F32)
    kv_b, dq = attend(core, rows, keys_b, BF, dq)
    kv_c, query_grad, query_sib = attend(core, rows, keys_c, F32, dq, last=True)
    kv_b = across(kv_b, 1)
    kv_a, kv_b, kv_c = lax.optimization_barrier((kv_a, kv_b, kv_c))
    kv_b = kv_b.astype(F32)
    kv_a, kv_c = kv_a + kv_b[:2], (kv_c + kv_b[2:]).astype(BF)
    kv_parts = [
        across(kv_a[1].astype(BF), 4),
        across(kv_c[0], 2),
        across(kv_c[1], 6),
    ]
    got, kv_parts, query_sib = lax.optimization_barrier((got, kv_parts, query_sib))
    query_sib = swap(query_sib[None])

    dots, w_down_grad, w_part = experts(core, got, swap(got[:, :, HALF:]), w_down, w_sib)
    dots = dots + swap(dots)
    dots = jnp.transpose(dots.reshape(LOCAL, NP, CAP), (1, 0, 2)).reshape(NP, 1, SLOTS)
    dots = jnp.broadcast_to(dots, (NP, NZ, SLOTS)).reshape(NP * NZ, SLOTS)
    kv_sum = kv_a[0]
    for part in kv_parts:
        kv_sum = kv_sum + part.astype(F32)
    dots = lax.all_to_all(dots, ("prompt", "z"), 0, 0, tiled=True)
    w_part = swap(w_part)
    query_grad = join(
        core,
        query_grad,
        query_sib,
        (2,),
        (1, HD, GROUP * HD // 2),
        lambda i, c: (0, 0, 2 * (1 - c[0]) + i),
        lambda i, c: (0, 0, i),
        "join_query",
    )
    w_down_grad = join(
        core,
        w_down_grad,
        w_part,
        (2,),
        (2, HALF, WID),
        lambda e, c: (e, 1 - c[0], 0),
        lambda e, c: (e, 0, 0),
        "join_down",
    )
    kv_mine, kv_back = kv_sum[:, :HD], swap(kv_sum[:, HD:])
    prompt_kv_grad = jnp.where(
        c == 0,
        jnp.concatenate([kv_mine, kv_back], axis=2),
        jnp.concatenate([kv_back, kv_mine], axis=2),
    )[None]
    dots, query_grad, w_down_grad = lax.optimization_barrier((dots, query_grad, w_down_grad))
    route_grad = collect(slot, weight_cols, dots).T
    return (query_grad, prompt_kv_grad, w_down_grad, route_grad)


def solution(mesh):
    cores = Mesh(mesh.devices.reshape(NP, NZ, 2), ("prompt", "z", "c"))
    member = ("z", "c")
    return jax.shard_map(
        body,
        mesh=cores,
        in_specs=(
            P("prompt", member, None),
            P("prompt", member, None),
            P("prompt", None, member),
            P("prompt", None, member),
            P("prompt", None, member, None),
            P("prompt", member),
            P("prompt", None, None),
            P("prompt", None),
            P("prompt", None),
            P("prompt", None, member),
        ),
        out_specs=(
            P("prompt", member, None),
            P("prompt", None, member, None),
            P("prompt", None, member),
            P("prompt", None),
        ),
        check_vma=False,
    )
```

```python
import functools
import math

import jax
import jax.numpy as jnp
from jax import lax
from jax.experimental import pallas as pl
from jax.experimental.pallas import tpu as pltpu
from jax.sharding import Mesh, PartitionSpec as P

QH = 32
KVH = 2
HD = 128
GROUP = QH // KVH
EFF = 1536
HALF = EFF // 2
TOPK = 8
CAP = 32
TOK = 128
ROUTES = TOK * TOPK
LOCAL = 4
EXPERTS = 64
SLOTS = LOCAL * CAP
DSTS = 4
NP = 16
NZ = 8
WID = 256
SCALE = HD ** (-0.5)
LOG2E = math.log2(math.e)
BF = jnp.bfloat16
F32 = jnp.float32
VMEM = 60 << 20
HEADS = 4
SWAP = [(0, 1), (1, 0)]


def shift(n, by):
    return [(i, (i + by) % n) for i in range(n)]


def cost(flops, moved, exps=0):
    return pl.CostEstimate(flops=flops, bytes_accessed=moved, transcendentals=exps)


def dot(a, b, ca=1, cb=0):
    return lax.dot_general(a, b, (((ca,), (cb,)), ((), ())), preferred_element_type=F32)


def iota(shape, dim):
    return lax.broadcasted_iota(jnp.int32, shape, dim)


def upper(n):
    return (iota((n, n), 0) < iota((n, n), 1)).astype(BF)


def dispatch_kernel(
    c_ref, ids_ref, w_ref, grad_ref, hid_ref, down_ref, out_ref, slot_ref, give_ref, row_ref
):
    give_ref[...] = down_ref[...]

    @pl.when(pl.program_id(0) == 0)
    def _():
        ids = ids_ref[...]
        hots = [(ids[k : k + 1] == iota((EXPERTS, TOK), 0)).astype(F32) for k in range(TOPK)]
        before = dot(sum(hots).astype(BF), upper(TOK))
        place = jnp.concatenate(
            [jnp.sum(h * before, axis=0, keepdims=True) for h in hots], axis=0
        )
        slot_ref[...] = ids * CAP + place.astype(jnp.int32)
        token = (iota((TOK, ROUTES), 0) == iota((TOK, ROUTES), 1) // TOPK).astype(F32).astype(BF)
        choice = (iota((TOPK, ROUTES), 0) == iota((TOPK, ROUTES), 1) % TOPK).astype(F32)
        wide = dot(ids.astype(F32).astype(BF), token) * CAP + dot(place.astype(BF), token)
        row_ref[...] = jnp.sum(wide * choice, axis=0, keepdims=True).astype(jnp.int32)

    slot = slot_ref[...]
    row = row_ref[...]
    weight = w_ref[...].astype(BF).astype(F32)
    for b in range(DSTS // 2):
        first = (pl.program_id(0) * DSTS + 2 * b) * SLOTS
        pick = (row == iota((2 * SLOTS, ROUTES), 0) + first).astype(F32).astype(BF)
        rows = dot(pick, hid_ref[...]).astype(BF)
        out_ref[2 * b : 2 * b + 2, :, :HALF] = rows.reshape(2, SLOTS, HALF)
        mine = iota((2 * SLOTS, TOK), 0) + first
        scale = jnp.zeros((2 * SLOTS, TOK), F32)
        for k in range(TOPK):
            scale = jnp.where(slot[k : k + 1] == mine, weight[k : k + 1], scale)
        scaled = dot(scale.astype(BF), grad_ref[...]).astype(BF)
        out_ref[2 * b : 2 * b + 2, :, HALF:] = scaled.reshape(2, SLOTS, WID)


def dispatch(core, ids_cols, weight_cols, grad_rows, hidden, w_down):
    small = pl.BlockSpec((TOPK, TOK), lambda j, c: (0, 0))
    return pl.pallas_call(
        dispatch_kernel,
        out_shape=(
            jax.ShapeDtypeStruct((NP, SLOTS, HALF + WID), BF),
            jax.ShapeDtypeStruct((TOPK, TOK), jnp.int32),
            jax.ShapeDtypeStruct((LOCAL, HALF, WID), BF),
        ),
        grid_spec=pltpu.PrefetchScalarGridSpec(
            num_scalar_prefetch=1,
            grid=(NP // DSTS,),
            in_specs=[
                small,
                small,
                pl.BlockSpec((TOK, WID), lambda j, c: (0, 0)),
                pl.BlockSpec((ROUTES, HALF), lambda j, c: (0, c[0])),
                pl.BlockSpec((1, HALF, WID), lambda j, c: (j, 1 - c[0], 0)),
            ],
            out_specs=(
                pl.BlockSpec((DSTS, SLOTS, HALF + WID), lambda j, c: (j, 0, 0)),
                small,
                pl.BlockSpec((1, HALF, WID), lambda j, c: (j, 0, 0)),
            ),
            scratch_shapes=[pltpu.VMEM((1, ROUTES), jnp.int32)],
        ),
        compiler_params=pltpu.CompilerParams(vmem_limit_bytes=VMEM),
        cost_estimate=cost(2 * NP * SLOTS * ROUTES * HALF, 6 << 20),
        name="dispatch",
    )(core, ids_cols, weight_cols, grad_rows, hidden, w_down)


def expert_kernel(c_ref, got_ref, ssib_ref, wown_ref, wsib_ref, dots_ref, own_ref, sib_ref):
    hid = got_ref[:, :, :HALF].reshape(NP * CAP, HALF)
    total = jnp.zeros((NP * CAP, HD), F32)
    for scl, w, out in (
        (got_ref[:, :, HALF:], wown_ref[0], own_ref),
        (ssib_ref[...], wsib_ref[0], sib_ref),
    ):
        scl = scl.reshape(NP * CAP, WID)
        prod = dot(hid, w) * scl.astype(F32)
        total = total + prod[:, :HD] + prod[:, HD:]
        out[0] = dot(hid, scl, 0, 0).astype(BF)
    dots_ref[0] = jnp.sum(total.T, axis=0, keepdims=True)


def experts(core, got, scl_sib, w_down, w_sib):
    half = pl.BlockSpec((1, HALF, WID), lambda e, c: (e, c[0], 0))
    return pl.pallas_call(
        expert_kernel,
        out_shape=(
            jax.ShapeDtypeStruct((LOCAL, 1, NP * CAP), F32),
            jax.ShapeDtypeStruct((LOCAL, EFF, WID), BF),
            jax.ShapeDtypeStruct((LOCAL, HALF, WID), BF),
        ),
        grid_spec=pltpu.PrefetchScalarGridSpec(
            num_scalar_prefetch=1,
            grid=(LOCAL,),
            in_specs=[
                pl.BlockSpec((NP, CAP, HALF + WID), lambda e, c: (0, e, 0)),
                pl.BlockSpec((NP, CAP, WID), lambda e, c: (0, e, 0)),
                half,
                pl.BlockSpec((1, HALF, WID), lambda e, c: (e, 0, 0)),
            ],
            out_specs=(
                pl.BlockSpec((1, 1, NP * CAP), lambda e, c: (e, 0, 0)),
                half,
                pl.BlockSpec((1, HALF, WID), lambda e, c: (e, 0, 0)),
            ),
        ),
        compiler_params=pltpu.CompilerParams(vmem_limit_bytes=VMEM),
        cost_estimate=cost(4 * LOCAL * 512 * HALF * 512, 13 << 20),
        name="experts",
    )(core, got, scl_sib, w_down, w_sib)


def join_kernel(c_ref, whole_ref, part_ref, out_ref):
    out_ref[...] = part_ref[...]


def join(core, whole, part, grid, block, whole_at, part_at, name):
    return pl.pallas_call(
        join_kernel,
        out_shape=jax.ShapeDtypeStruct(whole.shape, whole.dtype),
        grid_spec=pltpu.PrefetchScalarGridSpec(
            num_scalar_prefetch=1,
            grid=grid,
            in_specs=[pl.BlockSpec(memory_space=pl.ANY), pl.BlockSpec(block, part_at)],
            out_specs=pl.BlockSpec(block, whole_at),
        ),
        input_output_aliases={1: 0},
        compiler_params=pltpu.CompilerParams(vmem_limit_bytes=8 << 20),
        cost_estimate=cost(0, 2 * part.size * 2),
        name=name,
    )(core, whole, part)


def attend_kernel(first, last, *refs):
    c_ref, q_own, q_sib, g_own, g_sib, n_own, n_sib, d_own, d_sib, chunks = refs[:10]
    refs = refs[10:]
    if not first:
        dq_in, refs = refs[0], refs[1:]
    if last:
        dkv_out, dq_own, dq_sib, acc = refs
    else:
        dkv_out, dq_out, acc = refs
    step = pl.program_id(0)

    @pl.when(step == 0)
    def _():
        acc[...] = jnp.zeros_like(acc)

    heads = range(HEADS)
    cols = [slice(i * HD, (i + 1) * HD) for i in heads]
    q = jnp.concatenate([r[0, :, s] for s in cols for r in (q_own, q_sib)], axis=0)
    g = jnp.concatenate([r[0, :, s] for s in cols for r in (g_own, g_sib)], axis=0)

    def rows(own, sib):
        parts = []
        for i in heads:
            h = c_ref[0] * GROUP + step * HEADS + i
            parts += [own[0, pl.ds(h, 1), :], sib[0, pl.ds(h, 1), :]]
        return jnp.concatenate(parts, axis=1)

    norm = rows(n_own, n_sib) * LOG2E - math.log2(SCALE)
    delta = rows(d_own, d_sib)
    total = None
    for i in range(chunks.shape[0]):
        k, v = chunks[i, 0], chunks[i, 1]
        probs = jnp.exp2(dot(k, q, 1, 1) * (SCALE * LOG2E) - norm)
        dscore = (probs * (dot(v, g, 1, 1) - delta)).astype(BF)
        acc[i, 0] += dot(dscore, q)
        acc[i, 1] += dot(probs.astype(BF), g)
        term = dot(k, dscore, 0, 0)
        total = term if total is None else total + term
    total = total.T
    for i in heads:
        piece = total[i * 2 * HD : (i + 1) * 2 * HD]
        if not first:
            piece = piece + dq_in[:, cols[i]]
        if last:
            dq_own[0, :, cols[i]] = piece[:HD].astype(BF)
            dq_sib[:, cols[i]] = piece[HD:].astype(BF)
        else:
            dq_out[:, cols[i]] = piece

    @pl.when(step == GROUP // HEADS - 1)
    def _():
        dkv_out[:, 0] = acc[:, 0].astype(dkv_out.dtype)
        dkv_out[:, 1] = (acc[:, 1] * (1.0 / SCALE)).astype(dkv_out.dtype)


def attend(core, rows, chunks, kind, dq=None, last=False):
    first = dq is None
    count = chunks.shape[0]
    span = HEADS * HD
    wide = pl.BlockSpec((1, HD, span), lambda h, c: (0, 0, c[0] * (GROUP // HEADS) + h))
    line = pl.BlockSpec((1, QH, HD), lambda h, c: (0, 0, 0))
    keys = pl.BlockSpec(chunks.shape, lambda h, c: (0, 0, 0, 0))
    both = pl.BlockSpec((2 * HD, span), lambda h, c: (0, h))
    one = pl.BlockSpec((HD, span), lambda h, c: (0, h))
    in_specs = [wide] * 4 + [line] * 4 + [keys]
    args = [arr for pair in rows for arr in pair] + [chunks]
    outs = [jax.ShapeDtypeStruct(chunks.shape, kind)]
    out_specs = [keys]
    if not first:
        in_specs.append(both)
        args.append(dq)
    if last:
        outs += [
            jax.ShapeDtypeStruct((1, HD, QH * HD), BF),
            jax.ShapeDtypeStruct((HD, GROUP * HD), BF),
        ]
        out_specs += [wide, one]
    else:
        outs += [jax.ShapeDtypeStruct((2 * HD, GROUP * HD), F32)]
        out_specs += [both]
    return pl.pallas_call(
        functools.partial(attend_kernel, first, last),
        out_shape=tuple(outs),
        grid_spec=pltpu.PrefetchScalarGridSpec(
            num_scalar_prefetch=1,
            grid=(GROUP // HEADS,),
            in_specs=in_specs,
            out_specs=tuple(out_specs),
            scratch_shapes=[pltpu.VMEM(chunks.shape, F32)],
        ),
        compiler_params=pltpu.CompilerParams(vmem_limit_bytes=VMEM),
        cost_estimate=cost(
            10 * count * GROUP * 256 * 256 * 256, 8 << 20, count * GROUP * 256 * 256
        ),
        name=f"attend_{count}",
    )(core, *args)


def collect_kernel(slot_ref, w_ref, got_ref, out_ref):
    turned = jnp.sum(got_ref[...].reshape(NP, 2 * NZ, SLOTS), axis=1).T
    for k in range(TOPK):
        slot = slot_ref[k : k + 1, :]
        total = jnp.zeros((8, TOK), F32)
        for p in range(NP):
            want = iota((SLOTS, TOK), 0) + p * SLOTS
            hit = jnp.where(slot == want, turned[:, p : p + 1], 0.0)
            total = total + jnp.sum(hit.reshape(SLOTS // 8, 8, TOK), axis=0)
        out_ref[k : k + 1, :] = jnp.sum(total, axis=0, keepdims=True)
    out_ref[...] = out_ref[...] / w_ref[...].astype(BF).astype(F32)


def collect(slot, weight_cols, got):
    return pl.pallas_call(
        collect_kernel,
        out_shape=jax.ShapeDtypeStruct((TOPK, TOK), F32),
        compiler_params=pltpu.CompilerParams(vmem_limit_bytes=VMEM),
        cost_estimate=cost(8 << 20, 1 << 18),
        name="collect",
    )(slot, weight_cols, got)


def body(
    queries,
    out_grad,
    log_norms,
    row_deltas,
    prompt_kv,
    grad_rows,
    hidden_acts,
    route_weight,
    expert_ids,
    w_down,
):
    c = lax.axis_index("c")
    core = c.astype(jnp.int32)[None]
    prompt = lax.axis_index("prompt").astype(jnp.int32)[None]

    def swap(x):
        return lax.ppermute(x, "c", SWAP)

    def across(x, by):
        return lax.ppermute(x, "z", [(i, i ^ by) for i in range(NZ)])

    own = jnp.concatenate([prompt_kv[0], swap(prompt_kv[0])], axis=1)
    own = jnp.where(c == 0, own[:, :, :HD], own[:, :, HD:])[None]

    ids_cols, weight_cols = expert_ids.T, route_weight.T
    sent, slot, w_give = dispatch(
        core, ids_cols, weight_cols, grad_rows, hidden_acts.reshape(ROUTES, EFF), w_down
    )
    sibs = [swap(x) for x in (queries, out_grad, log_norms, row_deltas)]
    sent, sibs, own = lax.optimization_barrier((sent, sibs, own))
    rows = list(zip((queries, out_grad, log_norms, row_deltas), sibs))
    got = lax.all_to_all(sent, "prompt", 0, 0, tiled=True)
    keys = [own] + [across(own, k) for k in (4, 2, 6)]
    keys_a = jnp.concatenate(keys[:2], axis=0)
    keys_c = jnp.concatenate(keys[2:], axis=0)
    keys_b = across(jnp.concatenate([keys_a, keys_c], axis=0), 1)
    w_sib = swap(w_give)

    kv_a, dq = attend(core, rows, keys_a, F32)
    kv_b, dq = attend(core, rows, keys_b, BF, dq)
    kv_c, query_grad, query_sib = attend(core, rows, keys_c, F32, dq, last=True)
    kv_b = across(kv_b, 1)
    kv_a, kv_b, kv_c = lax.optimization_barrier((kv_a, kv_b, kv_c))
    kv_b = kv_b.astype(F32)
    kv_a, kv_c = kv_a + kv_b[:2], (kv_c + kv_b[2:]).astype(BF)
    got, kv_a, kv_c, query_sib = lax.optimization_barrier((got, kv_a, kv_c, query_sib))
    kv_parts = [
        across(kv_a[1].astype(BF), 4),
        across(kv_c[0], 2),
        across(kv_c[1], 6),
    ]
    query_sib = swap(query_sib[None])

    dots, w_down_grad, w_part = experts(core, got, swap(got[:, :, HALF:]), w_down, w_sib)
    dots = jnp.transpose(dots.reshape(LOCAL, NP, CAP), (1, 0, 2)).reshape(NP, 1, SLOTS)
    dots = jnp.broadcast_to(dots, (NP, 2 * NZ, SLOTS)).reshape(NP * 2 * NZ, SLOTS)
    dots = lax.all_to_all(dots, ("prompt", "z", "c"), 0, 0, tiled=True)
    w_part = swap(w_part)
    dots, kv_parts = lax.optimization_barrier((dots, kv_parts))
    kv_sum = kv_a[0]
    for part in kv_parts:
        kv_sum = kv_sum + part.astype(F32)
    query_grad = join(
        core,
        query_grad,
        query_sib,
        (2,),
        (1, HD, GROUP * HD // 2),
        lambda i, c: (0, 0, 2 * (1 - c[0]) + i),
        lambda i, c: (0, 0, i),
        "join_query",
    )
    w_down_grad = join(
        core,
        w_down_grad,
        w_part,
        (2,),
        (2, HALF, WID),
        lambda e, c: (e, 1 - c[0], 0),
        lambda e, c: (e, 0, 0),
        "join_down",
    )
    kv_mine, kv_back = kv_sum[:, :HD], swap(kv_sum[:, HD:])
    prompt_kv_grad = jnp.where(
        c == 0,
        jnp.concatenate([kv_mine, kv_back], axis=2),
        jnp.concatenate([kv_back, kv_mine], axis=2),
    )[None]
    dots, query_grad, w_down_grad = lax.optimization_barrier((dots, query_grad, w_down_grad))
    route_grad = collect(slot, weight_cols, dots).T
    return (query_grad, prompt_kv_grad, w_down_grad, route_grad)


def solution(mesh):
    cores = Mesh(mesh.devices.reshape(NP, NZ, 2), ("prompt", "z", "c"))
    member = ("z", "c")
    return jax.shard_map(
        body,
        mesh=cores,
        in_specs=(
            P("prompt", member, None),
            P("prompt", member, None),
            P("prompt", None, member),
            P("prompt", None, member),
            P("prompt", None, member, None),
            P("prompt", member),
            P("prompt", None, None),
            P("prompt", None),
            P("prompt", None),
            P("prompt", None, member),
        ),
        out_specs=(
            P("prompt", member, None),
            P("prompt", None, member, None),
            P("prompt", None, member),
            P("prompt", None),
        ),
        check_vma=False,
    )
```

```python
import functools
import math

import jax
import jax.numpy as jnp
from jax import lax
from jax.experimental import pallas as pl
from jax.experimental.pallas import tpu as pltpu
from jax.sharding import Mesh, PartitionSpec as P

QH = 32
KVH = 2
HD = 128
GROUP = QH // KVH
EFF = 1536
HALF = EFF // 2
TOPK = 8
CAP = 32
TOK = 128
ROUTES = TOK * TOPK
LOCAL = 4
EXPERTS = 64
SLOTS = LOCAL * CAP
DSTS = 4
NP = 16
NZ = 8
WID = 256
SCALE = HD ** (-0.5)
LOG2E = math.log2(math.e)
BF = jnp.bfloat16
F32 = jnp.float32
VMEM = 60 << 20
HEADS = 4
SWAP = [(0, 1), (1, 0)]


def shift(n, by):
    return [(i, (i + by) % n) for i in range(n)]


def cost(flops, moved, exps=0):
    return pl.CostEstimate(flops=flops, bytes_accessed=moved, transcendentals=exps)


def dot(a, b, ca=1, cb=0):
    return lax.dot_general(a, b, (((ca,), (cb,)), ((), ())), preferred_element_type=F32)


def iota(shape, dim):
    return lax.broadcasted_iota(jnp.int32, shape, dim)


def upper(n):
    return (iota((n, n), 0) < iota((n, n), 1)).astype(BF)


def dispatch_kernel(
    c_ref, ids_ref, w_ref, grad_ref, hid_ref, down_ref, out_ref, slot_ref, give_ref, row_ref
):
    give_ref[...] = down_ref[...]

    @pl.when(pl.program_id(0) == 0)
    def _():
        ids = ids_ref[...]
        hots = [(ids[k : k + 1] == iota((EXPERTS, TOK), 0)).astype(F32) for k in range(TOPK)]
        before = dot(sum(hots).astype(BF), upper(TOK))
        place = jnp.concatenate(
            [jnp.sum(h * before, axis=0, keepdims=True) for h in hots], axis=0
        )
        slot_ref[...] = ids * CAP + place.astype(jnp.int32)
        token = (iota((TOK, ROUTES), 0) == iota((TOK, ROUTES), 1) // TOPK).astype(F32).astype(BF)
        choice = (iota((TOPK, ROUTES), 0) == iota((TOPK, ROUTES), 1) % TOPK).astype(F32)
        wide = dot(ids.astype(F32).astype(BF), token) * CAP + dot(place.astype(BF), token)
        row_ref[...] = jnp.sum(wide * choice, axis=0, keepdims=True).astype(jnp.int32)

    slot = slot_ref[...]
    row = row_ref[...]
    weight = w_ref[...].astype(BF).astype(F32)
    for b in range(DSTS // 2):
        first = (pl.program_id(0) * DSTS + 2 * b) * SLOTS
        pick = (row == iota((2 * SLOTS, ROUTES), 0) + first).astype(F32).astype(BF)
        rows = dot(pick, hid_ref[...]).astype(BF)
        out_ref[2 * b : 2 * b + 2, :, :HALF] = rows.reshape(2, SLOTS, HALF)
        mine = iota((2 * SLOTS, TOK), 0) + first
        scale = jnp.zeros((2 * SLOTS, TOK), F32)
        for k in range(TOPK):
            scale = jnp.where(slot[k : k + 1] == mine, weight[k : k + 1], scale)
        scaled = dot(scale.astype(BF), grad_ref[...]).astype(BF)
        out_ref[2 * b : 2 * b + 2, :, HALF:] = scaled.reshape(2, SLOTS, WID)


def dispatch(core, ids_cols, weight_cols, grad_rows, hidden, w_down):
    small = pl.BlockSpec((TOPK, TOK), lambda j, c: (0, 0))
    return pl.pallas_call(
        dispatch_kernel,
        out_shape=(
            jax.ShapeDtypeStruct((NP, SLOTS, HALF + WID), BF),
            jax.ShapeDtypeStruct((TOPK, TOK), jnp.int32),
            jax.ShapeDtypeStruct((LOCAL, HALF, WID), BF),
        ),
        grid_spec=pltpu.PrefetchScalarGridSpec(
            num_scalar_prefetch=1,
            grid=(NP // DSTS,),
            in_specs=[
                small,
                small,
                pl.BlockSpec((TOK, WID), lambda j, c: (0, 0)),
                pl.BlockSpec((ROUTES, HALF), lambda j, c: (0, c[0])),
                pl.BlockSpec((1, HALF, WID), lambda j, c: (j, 1 - c[0], 0)),
            ],
            out_specs=(
                pl.BlockSpec((DSTS, SLOTS, HALF + WID), lambda j, c: (j, 0, 0)),
                small,
                pl.BlockSpec((1, HALF, WID), lambda j, c: (j, 0, 0)),
            ),
            scratch_shapes=[pltpu.VMEM((1, ROUTES), jnp.int32)],
        ),
        compiler_params=pltpu.CompilerParams(vmem_limit_bytes=VMEM),
        cost_estimate=cost(2 * NP * SLOTS * ROUTES * HALF, 6 << 20),
        name="dispatch",
    )(core, ids_cols, weight_cols, grad_rows, hidden, w_down)


def expert_kernel(c_ref, got_ref, ssib_ref, wown_ref, wsib_ref, dots_ref, own_ref, sib_ref):
    hid = got_ref[:, :, :HALF].reshape(NP * CAP, HALF)
    total = jnp.zeros((NP * CAP, HD), F32)
    for scl, w, out in (
        (got_ref[:, :, HALF:], wown_ref[0], own_ref),
        (ssib_ref[...], wsib_ref[0], sib_ref),
    ):
        scl = scl.reshape(NP * CAP, WID)
        prod = dot(hid, w) * scl.astype(F32)
        total = total + prod[:, :HD] + prod[:, HD:]
        out[0] = dot(hid, scl, 0, 0).astype(BF)
    dots_ref[0] = jnp.sum(total.T, axis=0, keepdims=True)


def experts(core, got, scl_sib, w_down, w_sib):
    half = pl.BlockSpec((1, HALF, WID), lambda e, c: (e, c[0], 0))
    return pl.pallas_call(
        expert_kernel,
        out_shape=(
            jax.ShapeDtypeStruct((LOCAL, 1, NP * CAP), F32),
            jax.ShapeDtypeStruct((LOCAL, EFF, WID), BF),
            jax.ShapeDtypeStruct((LOCAL, HALF, WID), BF),
        ),
        grid_spec=pltpu.PrefetchScalarGridSpec(
            num_scalar_prefetch=1,
            grid=(LOCAL,),
            in_specs=[
                pl.BlockSpec((NP, CAP, HALF + WID), lambda e, c: (0, e, 0)),
                pl.BlockSpec((NP, CAP, WID), lambda e, c: (0, e, 0)),
                half,
                pl.BlockSpec((1, HALF, WID), lambda e, c: (e, 0, 0)),
            ],
            out_specs=(
                pl.BlockSpec((1, 1, NP * CAP), lambda e, c: (e, 0, 0)),
                half,
                pl.BlockSpec((1, HALF, WID), lambda e, c: (e, 0, 0)),
            ),
        ),
        compiler_params=pltpu.CompilerParams(vmem_limit_bytes=VMEM),
        cost_estimate=cost(4 * LOCAL * 512 * HALF * 512, 13 << 20),
        name="experts",
    )(core, got, scl_sib, w_down, w_sib)


def join_kernel(c_ref, whole_ref, part_ref, out_ref):
    out_ref[...] = part_ref[...]


def join(core, whole, part, grid, block, whole_at, part_at, name):
    return pl.pallas_call(
        join_kernel,
        out_shape=jax.ShapeDtypeStruct(whole.shape, whole.dtype),
        grid_spec=pltpu.PrefetchScalarGridSpec(
            num_scalar_prefetch=1,
            grid=grid,
            in_specs=[pl.BlockSpec(memory_space=pl.ANY), pl.BlockSpec(block, part_at)],
            out_specs=pl.BlockSpec(block, whole_at),
        ),
        input_output_aliases={1: 0},
        compiler_params=pltpu.CompilerParams(vmem_limit_bytes=8 << 20),
        cost_estimate=cost(0, 2 * part.size * 2),
        name=name,
    )(core, whole, part)


def attend_kernel(first, last, *refs):
    c_ref, q_own, q_sib, g_own, g_sib, n_own, n_sib, d_own, d_sib, chunks = refs[:10]
    refs = refs[10:]
    if not first:
        dq_in, refs = refs[0], refs[1:]
    if last:
        dkv_out, dq_own, dq_sib, acc = refs
    else:
        dkv_out, dq_out, acc = refs
    step = pl.program_id(0)

    @pl.when(step == 0)
    def _():
        acc[...] = jnp.zeros_like(acc)

    heads = range(HEADS)
    cols = [slice(i * HD, (i + 1) * HD) for i in heads]
    q = jnp.concatenate([r[0, :, s] for s in cols for r in (q_own, q_sib)], axis=0)
    g = jnp.concatenate([r[0, :, s] for s in cols for r in (g_own, g_sib)], axis=0)

    def rows(own, sib):
        parts = []
        for i in heads:
            h = c_ref[0] * GROUP + step * HEADS + i
            parts += [own[0, pl.ds(h, 1), :], sib[0, pl.ds(h, 1), :]]
        return jnp.concatenate(parts, axis=1)

    norm = rows(n_own, n_sib) * LOG2E - math.log2(SCALE)
    delta = rows(d_own, d_sib)
    total = None
    for i in range(chunks.shape[0]):
        k, v = chunks[i, 0], chunks[i, 1]
        probs = jnp.exp2(dot(k, q, 1, 1) * (SCALE * LOG2E) - norm)
        dscore = (probs * (dot(v, g, 1, 1) - delta)).astype(BF)
        acc[i, 0] += dot(dscore, q)
        acc[i, 1] += dot(probs.astype(BF), g)
        term = dot(k, dscore, 0, 0)
        total = term if total is None else total + term
    total = total.T
    for i in heads:
        piece = total[i * 2 * HD : (i + 1) * 2 * HD]
        if not first:
            piece = piece + dq_in[:, cols[i]]
        if last:
            dq_own[0, :, cols[i]] = piece[:HD].astype(BF)
            dq_sib[:, cols[i]] = piece[HD:].astype(BF)
        else:
            dq_out[:, cols[i]] = piece

    @pl.when(step == GROUP // HEADS - 1)
    def _():
        dkv_out[:, 0] = acc[:, 0].astype(dkv_out.dtype)
        dkv_out[:, 1] = (acc[:, 1] * (1.0 / SCALE)).astype(dkv_out.dtype)


def attend(core, rows, chunks, kind, dq=None, last=False):
    first = dq is None
    count = chunks.shape[0]
    span = HEADS * HD
    wide = pl.BlockSpec((1, HD, span), lambda h, c: (0, 0, c[0] * (GROUP // HEADS) + h))
    line = pl.BlockSpec((1, QH, HD), lambda h, c: (0, 0, 0))
    keys = pl.BlockSpec(chunks.shape, lambda h, c: (0, 0, 0, 0))
    both = pl.BlockSpec((2 * HD, span), lambda h, c: (0, h))
    one = pl.BlockSpec((HD, span), lambda h, c: (0, h))
    in_specs = [wide] * 4 + [line] * 4 + [keys]
    args = [arr for pair in rows for arr in pair] + [chunks]
    outs = [jax.ShapeDtypeStruct(chunks.shape, kind)]
    out_specs = [keys]
    if not first:
        in_specs.append(both)
        args.append(dq)
    if last:
        outs += [
            jax.ShapeDtypeStruct((1, HD, QH * HD), BF),
            jax.ShapeDtypeStruct((HD, GROUP * HD), BF),
        ]
        out_specs += [wide, one]
    else:
        outs += [jax.ShapeDtypeStruct((2 * HD, GROUP * HD), F32)]
        out_specs += [both]
    return pl.pallas_call(
        functools.partial(attend_kernel, first, last),
        out_shape=tuple(outs),
        grid_spec=pltpu.PrefetchScalarGridSpec(
            num_scalar_prefetch=1,
            grid=(GROUP // HEADS,),
            in_specs=in_specs,
            out_specs=tuple(out_specs),
            scratch_shapes=[pltpu.VMEM(chunks.shape, F32)],
        ),
        compiler_params=pltpu.CompilerParams(vmem_limit_bytes=VMEM),
        cost_estimate=cost(
            10 * count * GROUP * 256 * 256 * 256, 8 << 20, count * GROUP * 256 * 256
        ),
        name=f"attend_{count}",
    )(core, *args)


def collect_kernel(slot_ref, w_ref, got_ref, out_ref):
    turned = jnp.sum(got_ref[...].reshape(NP, 2 * NZ, SLOTS), axis=1).T
    for k in range(TOPK):
        slot = slot_ref[k : k + 1, :]
        total = jnp.zeros((8, TOK), F32)
        for p in range(NP):
            want = iota((SLOTS, TOK), 0) + p * SLOTS
            hit = jnp.where(slot == want, turned[:, p : p + 1], 0.0)
            total = total + jnp.sum(hit.reshape(SLOTS // 8, 8, TOK), axis=0)
        out_ref[k : k + 1, :] = jnp.sum(total, axis=0, keepdims=True)
    out_ref[...] = out_ref[...] / w_ref[...].astype(BF).astype(F32)


def collect(slot, weight_cols, got):
    return pl.pallas_call(
        collect_kernel,
        out_shape=jax.ShapeDtypeStruct((TOPK, TOK), F32),
        compiler_params=pltpu.CompilerParams(vmem_limit_bytes=VMEM),
        cost_estimate=cost(8 << 20, 1 << 18),
        name="collect",
    )(slot, weight_cols, got)


def body(
    queries,
    out_grad,
    log_norms,
    row_deltas,
    prompt_kv,
    grad_rows,
    hidden_acts,
    route_weight,
    expert_ids,
    w_down,
):
    c = lax.axis_index("c")
    core = c.astype(jnp.int32)[None]
    prompt = lax.axis_index("prompt").astype(jnp.int32)[None]

    def swap(x):
        return lax.ppermute(x, "c", SWAP)

    def across(x, by):
        return lax.ppermute(x, "z", [(i, i ^ by) for i in range(NZ)])

    own = jnp.concatenate([prompt_kv[0], swap(prompt_kv[0])], axis=1)
    own = jnp.where(c == 0, own[:, :, :HD], own[:, :, HD:])[None]

    ids_cols, weight_cols = expert_ids.T, route_weight.T
    sent, slot, w_give = dispatch(
        core, ids_cols, weight_cols, grad_rows, hidden_acts.reshape(ROUTES, EFF), w_down
    )
    sibs = [swap(x) for x in (queries, out_grad, log_norms, row_deltas)]
    sent, sibs, own = lax.optimization_barrier((sent, sibs, own))
    rows = list(zip((queries, out_grad, log_norms, row_deltas), sibs))
    got = lax.all_to_all(sent, "prompt", 0, 0, tiled=True)
    near = [across(own, k) for k in (4, 2, 6)]
    w_sib = swap(w_give)

    kv_own, dq = attend(core, rows, own, F32)
    near, dq = lax.optimization_barrier((near, dq))
    far = across(jnp.concatenate([own] + near, axis=0), 1)
    kv_near, dq = attend(core, rows, jnp.concatenate(near, axis=0), F32, dq)
    kv_far, query_grad, query_sib = attend(core, rows, far, BF, dq, last=True)
    kv_far = across(kv_far, 1).astype(F32)
    kv_low = (kv_near + kv_far[1:]).astype(BF)
    kv_parts = [across(kv_low[i], k) for i, k in enumerate((4, 2, 6))]
    got, kv_parts, query_sib = lax.optimization_barrier((got, kv_parts, query_sib))
    query_sib = swap(query_sib[None])

    dots, w_down_grad, w_part = experts(core, got, swap(got[:, :, HALF:]), w_down, w_sib)
    dots = jnp.transpose(dots.reshape(LOCAL, NP, CAP), (1, 0, 2)).reshape(NP, 1, SLOTS)
    dots = jnp.broadcast_to(dots, (NP, 2 * NZ, SLOTS)).reshape(NP * 2 * NZ, SLOTS)
    dots = lax.all_to_all(dots, ("prompt", "z", "c"), 0, 0, tiled=True)
    w_part = swap(w_part)
    kv_sum = kv_own[0] + kv_far[0]
    for part in kv_parts:
        kv_sum = kv_sum + part.astype(F32)
    query_grad = join(
        core,
        query_grad,
        query_sib,
        (2,),
        (1, HD, GROUP * HD // 2),
        lambda i, c: (0, 0, 2 * (1 - c[0]) + i),
        lambda i, c: (0, 0, i),
        "join_query",
    )
    w_down_grad = join(
        core,
        w_down_grad,
        w_part,
        (2,),
        (2, HALF, WID),
        lambda e, c: (e, 1 - c[0], 0),
        lambda e, c: (e, 0, 0),
        "join_down",
    )
    kv_mine, kv_back = kv_sum[:, :HD], swap(kv_sum[:, HD:])
    prompt_kv_grad = jnp.where(
        c == 0,
        jnp.concatenate([kv_mine, kv_back], axis=2),
        jnp.concatenate([kv_back, kv_mine], axis=2),
    )[None]
    dots, query_grad, w_down_grad = lax.optimization_barrier((dots, query_grad, w_down_grad))
    route_grad = collect(slot, weight_cols, dots).T
    return (query_grad, prompt_kv_grad, w_down_grad, route_grad)


def solution(mesh):
    cores = Mesh(mesh.devices.reshape(NP, NZ, 2), ("prompt", "z", "c"))
    member = ("z", "c")
    return jax.shard_map(
        body,
        mesh=cores,
        in_specs=(
            P("prompt", member, None),
            P("prompt", member, None),
            P("prompt", None, member),
            P("prompt", None, member),
            P("prompt", None, member, None),
            P("prompt", member),
            P("prompt", None, None),
            P("prompt", None),
            P("prompt", None),
            P("prompt", None, member),
        ),
        out_specs=(
            P("prompt", member, None),
            P("prompt", None, member, None),
            P("prompt", None, member),
            P("prompt", None),
        ),
        check_vma=False,
    )
```

```python
import functools
import math

import jax
import jax.numpy as jnp
from jax import lax
from jax.experimental import pallas as pl
from jax.experimental.pallas import tpu as pltpu
from jax.sharding import Mesh, PartitionSpec as P

QH = 32
KVH = 2
HD = 128
GROUP = QH // KVH
EFF = 1536
HALF = EFF // 2
TOPK = 8
CAP = 32
TOK = 128
ROUTES = TOK * TOPK
LOCAL = 4
EXPERTS = 64
SLOTS = LOCAL * CAP
DSTS = 4
NP = 16
NZ = 8
WID = 256
SCALE = HD ** (-0.5)
LOG2E = math.log2(math.e)
BF = jnp.bfloat16
F32 = jnp.float32
VMEM = 60 << 20
HEADS = 4
SWAP = [(0, 1), (1, 0)]


def shift(n, by):
    return [(i, (i + by) % n) for i in range(n)]


def cost(flops, moved, exps=0):
    return pl.CostEstimate(flops=flops, bytes_accessed=moved, transcendentals=exps)


def dot(a, b, ca=1, cb=0):
    return lax.dot_general(a, b, (((ca,), (cb,)), ((), ())), preferred_element_type=F32)


def iota(shape, dim):
    return lax.broadcasted_iota(jnp.int32, shape, dim)


def upper(n):
    return (iota((n, n), 0) < iota((n, n), 1)).astype(BF)


def dispatch_kernel(
    c_ref, ids_ref, w_ref, grad_ref, hid_ref, down_ref, out_ref, slot_ref, give_ref, row_ref
):
    give_ref[...] = down_ref[...]

    @pl.when(pl.program_id(0) == 0)
    def _():
        ids = ids_ref[...]
        hots = [(ids[k : k + 1] == iota((EXPERTS, TOK), 0)).astype(F32) for k in range(TOPK)]
        before = dot(sum(hots).astype(BF), upper(TOK))
        place = jnp.concatenate(
            [jnp.sum(h * before, axis=0, keepdims=True) for h in hots], axis=0
        )
        slot_ref[...] = ids * CAP + place.astype(jnp.int32)
        token = (iota((TOK, ROUTES), 0) == iota((TOK, ROUTES), 1) // TOPK).astype(F32).astype(BF)
        choice = (iota((TOPK, ROUTES), 0) == iota((TOPK, ROUTES), 1) % TOPK).astype(F32)
        wide = dot(ids.astype(F32).astype(BF), token) * CAP + dot(place.astype(BF), token)
        row_ref[...] = jnp.sum(wide * choice, axis=0, keepdims=True).astype(jnp.int32)

    slot = slot_ref[...]
    row = row_ref[...]
    weight = w_ref[...].astype(BF).astype(F32)
    for b in range(DSTS // 2):
        first = (pl.program_id(0) * DSTS + 2 * b) * SLOTS
        pick = (row == iota((2 * SLOTS, ROUTES), 0) + first).astype(F32).astype(BF)
        rows = dot(pick, hid_ref[...]).astype(BF)
        out_ref[2 * b : 2 * b + 2, :, :HALF] = rows.reshape(2, SLOTS, HALF)
        mine = iota((2 * SLOTS, TOK), 0) + first
        scale = jnp.zeros((2 * SLOTS, TOK), F32)
        for k in range(TOPK):
            scale = jnp.where(slot[k : k + 1] == mine, weight[k : k + 1], scale)
        scaled = dot(scale.astype(BF), grad_ref[...]).astype(BF)
        out_ref[2 * b : 2 * b + 2, :, HALF:] = scaled.reshape(2, SLOTS, WID)


def dispatch(core, ids_cols, weight_cols, grad_rows, hidden, w_down):
    small = pl.BlockSpec((TOPK, TOK), lambda j, c: (0, 0))
    return pl.pallas_call(
        dispatch_kernel,
        out_shape=(
            jax.ShapeDtypeStruct((NP, SLOTS, HALF + WID), BF),
            jax.ShapeDtypeStruct((TOPK, TOK), jnp.int32),
            jax.ShapeDtypeStruct((LOCAL, HALF, WID), BF),
        ),
        grid_spec=pltpu.PrefetchScalarGridSpec(
            num_scalar_prefetch=1,
            grid=(NP // DSTS,),
            in_specs=[
                small,
                small,
                pl.BlockSpec((TOK, WID), lambda j, c: (0, 0)),
                pl.BlockSpec((ROUTES, HALF), lambda j, c: (0, c[0])),
                pl.BlockSpec((1, HALF, WID), lambda j, c: (j, 1 - c[0], 0)),
            ],
            out_specs=(
                pl.BlockSpec((DSTS, SLOTS, HALF + WID), lambda j, c: (j, 0, 0)),
                small,
                pl.BlockSpec((1, HALF, WID), lambda j, c: (j, 0, 0)),
            ),
            scratch_shapes=[pltpu.VMEM((1, ROUTES), jnp.int32)],
        ),
        compiler_params=pltpu.CompilerParams(vmem_limit_bytes=VMEM),
        cost_estimate=cost(2 * NP * SLOTS * ROUTES * HALF, 6 << 20),
        name="dispatch",
    )(core, ids_cols, weight_cols, grad_rows, hidden, w_down)


def expert_kernel(c_ref, got_ref, ssib_ref, wown_ref, wsib_ref, dots_ref, own_ref, sib_ref):
    hid = got_ref[:, :, :HALF].reshape(NP * CAP, HALF)
    total = jnp.zeros((NP * CAP, HD), F32)
    for scl, w, out in (
        (got_ref[:, :, HALF:], wown_ref[0], own_ref),
        (ssib_ref[...], wsib_ref[0], sib_ref),
    ):
        scl = scl.reshape(NP * CAP, WID)
        prod = dot(hid, w) * scl.astype(F32)
        total = total + prod[:, :HD] + prod[:, HD:]
        out[0] = dot(hid, scl, 0, 0).astype(BF)
    dots_ref[0] = jnp.sum(total.T, axis=0, keepdims=True)


def experts(core, got, scl_sib, w_down, w_sib):
    half = pl.BlockSpec((1, HALF, WID), lambda e, c: (e, c[0], 0))
    return pl.pallas_call(
        expert_kernel,
        out_shape=(
            jax.ShapeDtypeStruct((LOCAL, 1, NP * CAP), F32),
            jax.ShapeDtypeStruct((LOCAL, EFF, WID), BF),
            jax.ShapeDtypeStruct((LOCAL, HALF, WID), BF),
        ),
        grid_spec=pltpu.PrefetchScalarGridSpec(
            num_scalar_prefetch=1,
            grid=(LOCAL,),
            in_specs=[
                pl.BlockSpec((NP, CAP, HALF + WID), lambda e, c: (0, e, 0)),
                pl.BlockSpec((NP, CAP, WID), lambda e, c: (0, e, 0)),
                half,
                pl.BlockSpec((1, HALF, WID), lambda e, c: (e, 0, 0)),
            ],
            out_specs=(
                pl.BlockSpec((1, 1, NP * CAP), lambda e, c: (e, 0, 0)),
                half,
                pl.BlockSpec((1, HALF, WID), lambda e, c: (e, 0, 0)),
            ),
        ),
        compiler_params=pltpu.CompilerParams(vmem_limit_bytes=VMEM),
        cost_estimate=cost(4 * LOCAL * 512 * HALF * 512, 13 << 20),
        name="experts",
    )(core, got, scl_sib, w_down, w_sib)


def join_kernel(c_ref, whole_ref, part_ref, out_ref):
    out_ref[...] = part_ref[...]


def join(core, whole, part, grid, block, whole_at, part_at, name):
    return pl.pallas_call(
        join_kernel,
        out_shape=jax.ShapeDtypeStruct(whole.shape, whole.dtype),
        grid_spec=pltpu.PrefetchScalarGridSpec(
            num_scalar_prefetch=1,
            grid=grid,
            in_specs=[pl.BlockSpec(memory_space=pl.ANY), pl.BlockSpec(block, part_at)],
            out_specs=pl.BlockSpec(block, whole_at),
        ),
        input_output_aliases={1: 0},
        compiler_params=pltpu.CompilerParams(vmem_limit_bytes=8 << 20),
        cost_estimate=cost(0, 2 * part.size * 2),
        name=name,
    )(core, whole, part)


def attend_kernel(first, last, *refs):
    c_ref, q_own, q_sib, g_own, g_sib, n_own, n_sib, d_own, d_sib, chunks = refs[:10]
    refs = refs[10:]
    if not first:
        dq_in, refs = refs[0], refs[1:]
    if last:
        dkv_out, dq_own, dq_sib, acc = refs
    else:
        dkv_out, dq_out, acc = refs
    step = pl.program_id(0)

    @pl.when(step == 0)
    def _():
        acc[...] = jnp.zeros_like(acc)

    heads = range(HEADS)
    cols = [slice(i * HD, (i + 1) * HD) for i in heads]
    q = jnp.concatenate([r[0, :, s] for s in cols for r in (q_own, q_sib)], axis=0)
    g = jnp.concatenate([r[0, :, s] for s in cols for r in (g_own, g_sib)], axis=0)

    def rows(own, sib):
        parts = []
        for i in heads:
            h = c_ref[0] * GROUP + step * HEADS + i
            parts += [own[0, pl.ds(h, 1), :], sib[0, pl.ds(h, 1), :]]
        return jnp.concatenate(parts, axis=1)

    norm = rows(n_own, n_sib) * LOG2E - math.log2(SCALE)
    delta = rows(d_own, d_sib)
    total = None
    for i in range(chunks.shape[0]):
        k, v = chunks[i, 0], chunks[i, 1]
        probs = jnp.exp2(dot(k, q, 1, 1) * (SCALE * LOG2E) - norm)
        dscore = (probs * (dot(v, g, 1, 1) - delta)).astype(BF)
        acc[i, 0] += dot(dscore, q)
        acc[i, 1] += dot(probs.astype(BF), g)
        term = dot(k, dscore, 0, 0)
        total = term if total is None else total + term
    total = total.T
    for i in heads:
        piece = total[i * 2 * HD : (i + 1) * 2 * HD]
        if not first:
            piece = piece + dq_in[:, cols[i]]
        if last:
            dq_own[0, :, cols[i]] = piece[:HD].astype(BF)
            dq_sib[:, cols[i]] = piece[HD:].astype(BF)
        else:
            dq_out[:, cols[i]] = piece

    @pl.when(step == GROUP // HEADS - 1)
    def _():
        dkv_out[:, 0] = acc[:, 0].astype(dkv_out.dtype)
        dkv_out[:, 1] = (acc[:, 1] * (1.0 / SCALE)).astype(dkv_out.dtype)


def attend(core, rows, chunks, kind, dq=None, last=False):
    first = dq is None
    count = chunks.shape[0]
    span = HEADS * HD
    wide = pl.BlockSpec((1, HD, span), lambda h, c: (0, 0, c[0] * (GROUP // HEADS) + h))
    line = pl.BlockSpec((1, QH, HD), lambda h, c: (0, 0, 0))
    keys = pl.BlockSpec(chunks.shape, lambda h, c: (0, 0, 0, 0))
    both = pl.BlockSpec((2 * HD, span), lambda h, c: (0, h))
    one = pl.BlockSpec((HD, span), lambda h, c: (0, h))
    in_specs = [wide] * 4 + [line] * 4 + [keys]
    args = [arr for pair in rows for arr in pair] + [chunks]
    outs = [jax.ShapeDtypeStruct(chunks.shape, kind)]
    out_specs = [keys]
    if not first:
        in_specs.append(both)
        args.append(dq)
    if last:
        outs += [
            jax.ShapeDtypeStruct((1, HD, QH * HD), BF),
            jax.ShapeDtypeStruct((HD, GROUP * HD), BF),
        ]
        out_specs += [wide, one]
    else:
        outs += [jax.ShapeDtypeStruct((2 * HD, GROUP * HD), F32)]
        out_specs += [both]
    return pl.pallas_call(
        functools.partial(attend_kernel, first, last),
        out_shape=tuple(outs),
        grid_spec=pltpu.PrefetchScalarGridSpec(
            num_scalar_prefetch=1,
            grid=(GROUP // HEADS,),
            in_specs=in_specs,
            out_specs=tuple(out_specs),
            scratch_shapes=[pltpu.VMEM(chunks.shape, F32)],
        ),
        compiler_params=pltpu.CompilerParams(vmem_limit_bytes=VMEM),
        cost_estimate=cost(
            10 * count * GROUP * 256 * 256 * 256, 8 << 20, count * GROUP * 256 * 256
        ),
        name=f"attend_{count}",
    )(core, *args)


def collect_kernel(slot_ref, w_ref, got_ref, out_ref):
    turned = jnp.sum(got_ref[...].reshape(NP, 2 * NZ, SLOTS), axis=1).T
    for k in range(TOPK):
        slot = slot_ref[k : k + 1, :]
        total = jnp.zeros((8, TOK), F32)
        for p in range(NP):
            want = iota((SLOTS, TOK), 0) + p * SLOTS
            hit = jnp.where(slot == want, turned[:, p : p + 1], 0.0)
            total = total + jnp.sum(hit.reshape(SLOTS // 8, 8, TOK), axis=0)
        out_ref[k : k + 1, :] = jnp.sum(total, axis=0, keepdims=True)
    out_ref[...] = out_ref[...] / w_ref[...].astype(BF).astype(F32)


def collect(slot, weight_cols, got):
    return pl.pallas_call(
        collect_kernel,
        out_shape=jax.ShapeDtypeStruct((TOPK, TOK), F32),
        compiler_params=pltpu.CompilerParams(vmem_limit_bytes=VMEM),
        cost_estimate=cost(8 << 20, 1 << 18),
        name="collect",
    )(slot, weight_cols, got)


def body(
    queries,
    out_grad,
    log_norms,
    row_deltas,
    prompt_kv,
    grad_rows,
    hidden_acts,
    route_weight,
    expert_ids,
    w_down,
):
    c = lax.axis_index("c")
    core = c.astype(jnp.int32)[None]
    prompt = lax.axis_index("prompt").astype(jnp.int32)[None]

    def swap(x):
        return lax.ppermute(x, "c", SWAP)

    def across(x, by):
        return lax.ppermute(x, "z", [(i, i ^ by) for i in range(NZ)])

    own = jnp.concatenate([prompt_kv[0], swap(prompt_kv[0])], axis=1)
    own = jnp.where(c == 0, own[:, :, :HD], own[:, :, HD:])[None]

    ids_cols, weight_cols = expert_ids.T, route_weight.T
    sent, slot, w_give = dispatch(
        core, ids_cols, weight_cols, grad_rows, hidden_acts.reshape(ROUTES, EFF), w_down
    )
    sibs = [swap(x) for x in (queries, out_grad, log_norms, row_deltas)]
    sent, sibs, own = lax.optimization_barrier((sent, sibs, own))
    rows = list(zip((queries, out_grad, log_norms, row_deltas), sibs))
    got = lax.all_to_all(sent, "prompt", 0, 0, tiled=True)
    near = [across(own, k) for k in (4, 2, 6)]
    w_sib = swap(w_give)

    kv_own, dq = attend(core, rows, own, F32)
    near, dq = lax.optimization_barrier((near, dq))
    far = across(jnp.concatenate([own] + near, axis=0), 1)
    kv_near, dq = attend(core, rows, jnp.concatenate(near, axis=0), F32, dq)
    kv_far, query_grad, query_sib = attend(core, rows, far, BF, dq, last=True)
    kv_far = across(kv_far, 1).astype(F32)
    kv_low = (kv_near + kv_far[1:]).astype(BF)
    got, kv_low, query_sib = lax.optimization_barrier((got, kv_low, query_sib))
    kv_parts = [across(kv_low[i], k) for i, k in enumerate((4, 2, 6))]
    query_sib = swap(query_sib[None])

    dots, w_down_grad, w_part = experts(core, got, swap(got[:, :, HALF:]), w_down, w_sib)
    dots = jnp.transpose(dots.reshape(LOCAL, NP, CAP), (1, 0, 2)).reshape(NP, 1, SLOTS)
    dots = jnp.broadcast_to(dots, (NP, 2 * NZ, SLOTS)).reshape(NP * 2 * NZ, SLOTS)
    dots = lax.all_to_all(dots, ("prompt", "z", "c"), 0, 0, tiled=True)
    w_part = swap(w_part)
    dots, kv_parts = lax.optimization_barrier((dots, kv_parts))
    kv_sum = kv_own[0] + kv_far[0]
    for part in kv_parts:
        kv_sum = kv_sum + part.astype(F32)
    query_grad = join(
        core,
        query_grad,
        query_sib,
        (2,),
        (1, HD, GROUP * HD // 2),
        lambda i, c: (0, 0, 2 * (1 - c[0]) + i),
        lambda i, c: (0, 0, i),
        "join_query",
    )
    w_down_grad = join(
        core,
        w_down_grad,
        w_part,
        (2,),
        (2, HALF, WID),
        lambda e, c: (e, 1 - c[0], 0),
        lambda e, c: (e, 0, 0),
        "join_down",
    )
    kv_mine, kv_back = kv_sum[:, :HD], swap(kv_sum[:, HD:])
    prompt_kv_grad = jnp.where(
        c == 0,
        jnp.concatenate([kv_mine, kv_back], axis=2),
        jnp.concatenate([kv_back, kv_mine], axis=2),
    )[None]
    dots, query_grad, w_down_grad = lax.optimization_barrier((dots, query_grad, w_down_grad))
    route_grad = collect(slot, weight_cols, dots).T
    return (query_grad, prompt_kv_grad, w_down_grad, route_grad)


def solution(mesh):
    cores = Mesh(mesh.devices.reshape(NP, NZ, 2), ("prompt", "z", "c"))
    member = ("z", "c")
    return jax.shard_map(
        body,
        mesh=cores,
        in_specs=(
            P("prompt", member, None),
            P("prompt", member, None),
            P("prompt", None, member),
            P("prompt", None, member),
            P("prompt", None, member, None),
            P("prompt", member),
            P("prompt", None, None),
            P("prompt", None),
            P("prompt", None),
            P("prompt", None, member),
        ),
        out_specs=(
            P("prompt", member, None),
            P("prompt", None, member, None),
            P("prompt", None, member),
            P("prompt", None),
        ),
        check_vma=False,
    )
```
